128 devices in a mesh: seq: 16 (over z, x_lo, core), tp: 8 (over x_hi, y).
Axes of the slice: x: 4 (x_hi: 2, x_lo: 2; x = x_hi * 2 + x_lo), y: 4, z: 4, core: 2. Of those that a mesh axis runs over, the one named last changes fastest.
Arguments:
- tokens: bfloat16 [8192, 4096], P(('seq', 'tp')), may hold values from -6 to 6
- norm_gain: float32 [4096], replicated, may hold values from 0.1 to 1.9
- in_weight: bfloat16 [4096, 3, 4096], P('seq', None, 'tp'), may hold values from -0.09375 to 0.09375
- short_filter: float32 [7, 3, 4096], P(None, None, 'tp'), may hold values from -2.4 to 2.4
- long_filter: float32 [128, 4096], P(None, 'tp'), may hold values from -0.6 to 0.6
- skip_gain: float32 [4096], P('tp'), may hold values from -4 to 4
- out_weight: bfloat16 [4096, 4096], P('tp', 'seq'), may hold values from -0.09375 to 0.09375
Outputs:
- mixed: bfloat16 [8192, 4096], P(('seq', 'tp'))
The draws below stay inside these ranges and needn't reach their ends.
All inputs are finite; a program needn't handle non-finite values.
Results may differ from the reference program's by a relative error of at most 0.02.
Values may be sent and summed in bfloat16 or wider, within the bound.
A program may use at most 256 MiB of HBM per device.

```python
import jax
import jax.numpy as jnp
from jax import lax

D = 4096
FILT = 128
SHORT = 7
TOKENS = 8192


def draw_long_filter(key, part):
    key = jax.random.fold_in(key, 11)
    rate_key, tap_key = jax.random.split(key)
    rates = jnp.exp(jax.random.uniform(rate_key, (D,), jnp.float32, jnp.log(1.0 / 400.0), jnp.log(1.0 / 8.0)))
    lags = jnp.arange(FILT, dtype=jnp.float32)[:, None]
    base = jax.random.truncated_normal(tap_key, -4.0, 4.0, (FILT, D), jnp.float32)
    return (0.15 * base * jnp.exp(-rates * lags)).astype(jnp.float32)


def shard_levels(own_key, extent, shards, low, largest):
    loudness = 1.0
    for axis_at, blocks in shards:
        draws = jax.random.uniform(jax.random.fold_in(jax.random.fold_in(own_key, 6), axis_at), (blocks,), jnp.float32, low / len(shards), largest / len(shards))
        loudness = loudness * jnp.repeat(jnp.exp(draws), extent[axis_at] // blocks).reshape((-1,) + (1,) * (len(extent) - 1 - axis_at))
    return loudness


def normal_values(rng, extent, scale, most, shards=(), kind=jnp.bfloat16):
    entries = jax.random.normal(rng, extent, jnp.float32) * scale
    if len(shards) > 0:
        entries = shard_levels(rng, extent, shards, -0.22, 0.18) * entries
    return jnp.clip(entries, min=-most, max=most).astype(kind)


def setup_inputs(seed: int = 0) -> dict:
    arg_keys = jax.random.split(jax.random.key(seed), 8)
    tokens = normal_values(arg_keys[0], (TOKENS, D), 1.0, 6.0, ((0, 128),))
    norm_gain = jnp.clip(1.0 + 0.18 * jax.random.normal(arg_keys[1], (D,), jnp.float32), 0.1, 1.9)
    in_weight = normal_values(arg_keys[2], (D, 3, D), D ** -0.5, 0.09375, ((0, 16), (2, 8)))
    short_filter = normal_values(arg_keys[3], (SHORT, 3, D), 0.4, 2.4, ((2, 8),), jnp.float32)
    long_filter = draw_long_filter(jax.random.fold_in(arg_keys[7], 71), 0)
    skip_gain = normal_values(arg_keys[5], (D,), 1.0, 4.0, ((0, 8),), jnp.float32)
    out_weight = normal_values(arg_keys[6], (D, D), D ** -0.5, 0.09375, ((0, 8), (1, 16)))
    return dict(tokens=tokens, norm_gain=norm_gain, in_weight=in_weight, short_filter=short_filter, long_filter=long_filter, skip_gain=skip_gain, out_weight=out_weight)


def reference(tokens, norm_gain, in_weight, short_filter, long_filter, skip_gain, out_weight):
    widened = tokens.astype(jnp.float32)
    mean_square = lax.optimization_barrier(jnp.mean(widened * widened, axis=-1, keepdims=True))
    normed = (widened * lax.rsqrt(mean_square + 1e-06) * norm_gain).astype(jnp.bfloat16)
    length = tokens.shape[0]
    width = tokens.shape[1]
    branches = jnp.dot(normed, in_weight.reshape(width, 3 * width), preferred_element_type=jnp.float32)
    branches = branches.reshape(length, 3, width).astype(jnp.bfloat16).astype(jnp.float32)
    padded = jnp.pad(branches, ((SHORT - 1, 0), (0, 0), (0, 0)))
    featured = jnp.zeros((length, 3, width), jnp.float32)
    for delay in range(SHORT):
        featured = featured + short_filter[delay] * padded[SHORT - 1 - delay:SHORT - 1 - delay + length]
    gated = (featured[:, 1] * featured[:, 2]).astype(jnp.bfloat16).astype(jnp.float32)
    gated_pad = jnp.pad(gated, ((FILT - 1, 0), (0, 0)))

    def add_tap(index, total):
        lagged = lax.dynamic_slice_in_dim(gated_pad, FILT - 1 - index, length, 0)
        return total + long_filter[index] * lagged
    filtered = lax.fori_loop(0, FILT, add_tap, jnp.zeros((length, width), jnp.float32))
    filtered = filtered + skip_gain * gated
    mixed_in = (featured[:, 0] * filtered).astype(jnp.bfloat16)
    summed = jnp.dot(mixed_in, out_weight, preferred_element_type=jnp.float32)
    return (widened + summed).astype(jnp.bfloat16)
```

```python
import functools

import jax
import jax.numpy as jnp
from jax import lax
from jax.experimental import pallas as pl
from jax.experimental.pallas import tpu as pltpu
from jax.sharding import PartitionSpec as P

MESH = pl.DeviceIdType.MESH
BF16 = jnp.bfloat16
F32 = jnp.float32

CHUNKS = 4
LANES = 128
HALO = 144
Z_FIRST = (1,)


def in_proj(normed, weights, branches, k):
    rows = normed.shape[0]

    def body(i, carry):
        at = pl.multiple_of(i * 256, 256)
        out = jnp.dot(normed[pl.ds(at, 256), :], weights[k], preferred_element_type=F32)
        branches[k, pl.ds(pl.multiple_of(HALO + at, 16), 256), :] = out.astype(BF16)
        return carry

    lax.fori_loop(0, rows // 256, body, 0)


def featurize(branches, short_ref, wide, query, gate, k):
    total = branches.shape[1]
    block = total - HALO

    def widen(i, carry):
        at = pl.multiple_of(i * 16, 16)
        for p in range(3):
            wide[p, pl.ds(at, 16), :] = branches[k, pl.ds(at, 16), p * LANES : (p + 1) * LANES].astype(F32)
        return carry

    lax.fori_loop(0, total // 16, widen, 0)
    taps = [[short_ref[j, p, k * LANES : (k + 1) * LANES][None] for j in range(7)] for p in range(3)]

    def filt(p, first, rows):
        out = taps[p][0] * wide[p, pl.ds(first, rows), :]
        for j in range(1, 7):
            out = out + taps[p][j] * wide[p, pl.ds(first - j, rows), :]
        return out

    def gates(i, carry):
        at = pl.multiple_of(i * 32, 32)
        value = filt(1, 16 + at, 32) * filt(2, 16 + at, 32)
        gate[pl.ds(at, 32), :] = value.astype(BF16).astype(F32)
        return carry

    lax.fori_loop(0, (block + 128) // 32, gates, 0)

    def queries(i, carry):
        at = pl.multiple_of(i * 32, 32)
        query[pl.ds(at, 32), :] = filt(0, HALO + at, 32)
        return carry

    lax.fori_loop(0, block // 32, queries, 0)


def long_conv(gate, query, long_ref, skip_ref, mixed, k):
    columns = slice(k * LANES, (k + 1) * LANES)
    block = query.shape[0]
    tile = 64

    def body(i, carry):
        at = pl.multiple_of(i * tile, tile)
        total = (long_ref[0:1, columns] + skip_ref[:, columns]) * gate[pl.ds(128 + at, tile), :]
        for j in range(1, 128):
            total = total + long_ref[j : j + 1, columns] * gate[pl.ds(128 + at - j, tile), :]
        mixed[pl.ds(at, tile), columns] = (query[pl.ds(at, tile), :] * total).astype(BF16)
        return carry

    lax.fori_loop(0, block // tile, body, 0)


def kernel(
    tokens,
    gain,
    in_w,
    short_ref,
    long_ref,
    skip_ref,
    out_w,
    result,
    normed,
    weights,
    out_weights,
    branches,
    wide,
    query,
    gate,
    mixed,
    part,
    landed,
    send_sems,
    w_sems,
    t_sems,
    h_sems,
    r_sems,
    l_sems,
):
    s, t = lax.axis_index("seq"), lax.axis_index("tp")
    z, xl, core = s // 4, (s // 2) % 2, s % 2
    xh, y = t // 4, t % 4

    def on_seq(dz, dx, dc):
        return ((z + dz) % 4) * 4 + ((xl + dx) % 2) * 2 + (core + dc) % 2

    def on_tp(dx, dy):
        return ((xh + dx) % 2) * 4 + (y + dy) % 4

    def seq_device(dz, dx, dc):
        return (on_seq(dz, dx, dc), t)

    def tp_device(dx, dy):
        return (s, on_tp(dx, dy))

    after = (lax.rem(s + 1, 16), t)
    before = (lax.rem(s + 15, 16), t)
    sibling = seq_device(0, 0, 1)

    partners = [sibling, seq_device(0, 1, 0), seq_device(1, 0, 0), seq_device(3, 0, 0), after, before]
    partners += [tp_device(dx, dy) for dx in range(2) for dy in range(4) if dx or dy]
    barrier = pltpu.get_barrier_semaphore()
    for partner in partners:
        pl.semaphore_signal(barrier, inc=1, device_id=partner, device_id_type=MESH)

    started = []

    def send(src, dst, recv_sem, device):
        copy = pltpu.make_async_remote_copy(
            src_ref=src,
            dst_ref=dst,
            send_sem=send_sems.at[len(started)],
            recv_sem=recv_sem,
            device_id=device,
            device_id_type=MESH,
        )
        copy.start()
        started.append(copy)

    def arrived(dst, recv_sem):
        pltpu.make_async_remote_copy(
            src_ref=dst,
            dst_ref=dst,
            send_sem=send_sems.at[0],
            recv_sem=recv_sem,
            device_id=sibling,
            device_id_type=MESH,
        ).wait_recv()

    local = []
    for k in range(CHUNKS):
        local.append(pltpu.make_async_copy(in_w.at[k], weights.at[k, pl.ds(pl.multiple_of(s * 256, 256), 256)], l_sems.at[k]))
    local.append(pltpu.make_async_copy(out_w, out_weights.at[s], l_sems.at[CHUNKS]))
    for copy in local:
        copy.start()

    own_rows = pl.multiple_of(t * 64, 64)
    for i in range(4):
        rows = tokens[i * 16 : (i + 1) * 16, :].astype(F32)
        scale = lax.rsqrt(jnp.mean(rows * rows, axis=-1, keepdims=True) + 1e-06)
        normed[pl.ds(own_rows + i * 16, 16), :] = (rows * scale * gain[...]).astype(BF16)

    pl.semaphore_wait(barrier, len(partners))

    def token_rows(dx, dy, half=None):
        first = on_tp(dx, dy) * 64
        if half is None:
            return normed.at[pl.ds(pl.multiple_of(first, 64), 64)]
        return normed.at[pl.ds(pl.multiple_of(first + 32 * half, 32), 32)]

    def t_round(dx):
        rows = token_rows(dx, 0)
        send(rows, rows, t_sems.at[dx, 3, 0], tp_device(0, 1))
        send(rows, rows, t_sems.at[dx, 1, 0], tp_device(0, 3))

    def t_pass(dx):
        arrived(token_rows(dx, 3), t_sems.at[dx, 3, 0])
        send(token_rows(dx, 3, 0), token_rows(dx, 3, 0), t_sems.at[dx, 2, 0], tp_device(0, 1))
        arrived(token_rows(dx, 1), t_sems.at[dx, 1, 0])
        send(token_rows(dx, 1, 1), token_rows(dx, 1, 1), t_sems.at[dx, 2, 1], tp_device(0, 3))

    def t_last(dx):
        for half in range(2):
            arrived(token_rows(dx, 2, half), t_sems.at[dx, 2, half])

    def shard(k, dz, dx, dc=0, half=None):
        origin = on_seq(dz, dx, dc)
        if k < CHUNKS:
            ref, depth = weights.at[k], 256
            first = origin * 256
        else:
            ref, depth = out_weights.at[origin], 512
            first = 0
        if half is None:
            return ref.at[pl.ds(pl.multiple_of(first, 256), depth)]
        return ref.at[pl.ds(pl.multiple_of(first + half * (depth // 2), 128), depth // 2)]

    def w_send(k, dz, dx, device, slot_dz, slot_dx, index=0, half=None):
        ref = shard(k, dz, dx, 0, half)
        send(ref, ref, w_sems.at[k, slot_dz, slot_dx, index], device)

    def w_arrived(k, dz, dx):
        if dz == 2 and (dx == 0 or k not in Z_FIRST):
            for half in range(2):
                arrived(shard(k, dz, dx, 0, half), w_sems.at[k, dz, dx, half])
        else:
            arrived(shard(k, dz, dx), w_sems.at[k, dz, dx, 0])

    def w_sibling(k, dz, dx):
        w_send(k, dz, dx, sibling, dz, dx, 2)

    def w_along_x(k, dz):
        w_send(k, dz, 0, seq_device(0, 1, 0), dz, 1)

    def w_round(k, dx):
        w_send(k, 0, dx, seq_device(1, 0, 0), 3, dx)
        w_send(k, 0, dx, seq_device(3, 0, 0), 1, dx)

    def w_pass(k, dz, dx):
        half = 0 if dz == 3 else 1
        w_send(k, dz, dx, seq_device(4 - dz, 0, 0), 2, dx, half, half)

    def w_start(k):
        local[k].wait()
        w_along_x(k, 0)
        w_round(k, 0)
        w_sibling(k, 0, 0)

    def w_second(k):
        if k in Z_FIRST:
            for dz in (3, 1):
                w_arrived(k, dz, 0)
                w_pass(k, dz, 0)
                w_along_x(k, dz)
                w_sibling(k, dz, 0)
        else:
            w_arrived(k, 0, 1)
            w_round(k, 1)
            w_sibling(k, 0, 1)
            for dz in (3, 1):
                w_arrived(k, dz, 0)
                w_pass(k, dz, 0)
                w_sibling(k, dz, 0)

    def w_third(k):
        if k in Z_FIRST:
            w_arrived(k, 2, 0)
            w_along_x(k, 2)
            w_sibling(k, 2, 0)
        else:
            for dz in (3, 1):
                w_arrived(k, dz, 1)
                w_pass(k, dz, 1)
                w_sibling(k, dz, 1)

    def w_fourth(k):
        if k in Z_FIRST:
            for dz in (0, 3, 1, 2):
                w_arrived(k, dz, 1)
                w_sibling(k, dz, 1)
        else:
            for dx in range(2):
                w_arrived(k, 2, dx)
                w_sibling(k, 2, dx)

    def w_from_sibling(k, dz, dx):
        arrived(shard(k, dz, dx, 1), w_sems.at[k, dz, dx, 2])

    def w_ready(k):
        for dz in range(4):
            for dx in range(2):
                w_from_sibling(k, dz, dx)

    def halo_send(k):
        block = branches.shape[1] - HALO
        send(branches.at[k, pl.ds(block, HALO)], branches.at[k, pl.ds(0, HALO)], h_sems.at[k], after)

    def halo_wait(k):
        arrived(branches.at[k, pl.ds(0, HALO)], h_sems.at[k])

        @pl.when(s == 0)
        def _():
            branches[k, 0:HALO, :] = jnp.zeros((HALO, branches.shape[2]), BF16)

    def project(k):
        in_proj(normed, weights, branches, k)
        halo_send(k)

    def mix(k):
        halo_wait(k)
        featurize(branches, short_ref, wide, query, gate, k)
        long_conv(gate, query, long_ref, skip_ref, mixed, k)

    send(token_rows(0, 0), token_rows(0, 0), t_sems.at[1, 0, 0], tp_device(1, 0))
    t_round(0)
    w_start(0)
    w_start(1)
    arrived(token_rows(1, 0), t_sems.at[1, 0, 0])
    t_round(1)
    w_second(0)
    w_start(2)
    t_pass(0)
    w_third(0)
    w_second(1)
    w_start(3)
    w_fourth(0)
    w_third(1)
    w_second(2)
    t_pass(1)
    t_last(0)
    w_start(4)
    w_fourth(1)
    t_last(1)
    w_ready(0)
    project(0)
    w_third(2)
    w_second(3)
    mix(0)
    w_fourth(2)
    w_third(3)
    w_ready(1)
    project(1)
    w_fourth(3)
    w_second(4)
    mix(1)
    w_third(4)
    w_ready(2)
    project(2)
    w_ready(3)
    project(3)
    mix(2)
    w_fourth(4)
    mix(3)

    groups = [(0, 0), (0, 1), (3, 0), (1, 0), (3, 1), (1, 1), (2, 0), (2, 1)]
    others = [(dx, dy) for dy in (2, 1, 3, 0) for dx in (1, 0) if dx or dy]

    def columns_of(dz, dx):
        return pl.ds(pl.multiple_of(on_seq(dz, dx, 0) // 2 * 512, 512), 512)

    for g, (dz, dx) in enumerate(groups):
        w_from_sibling(4, dz, dx)
        first = (on_seq(dz, dx, 0) // 2) * 2

        def out_proj(i, carry, first=first):
            origin = first + i
            out = jnp.dot(mixed[...], out_weights[origin], preferred_element_type=F32)
            part[:, pl.ds(pl.multiple_of(origin * 256, 256), 256)] = out.astype(BF16)
            return carry

        lax.fori_loop(0, 2, out_proj, 0)
        columns = columns_of(dz, dx)
        for n, (tx, ty) in enumerate(others):
            rows = pl.ds(pl.multiple_of(on_tp(tx, ty) * 64, 64), 64)
            send(part.at[rows, columns], landed.at[n, :, columns], r_sems.at[g, n], tp_device(tx, ty))

    for g, (dz, dx) in enumerate(groups):
        columns = columns_of(dz, dx)
        for n in range(len(others)):
            arrived(landed.at[n, :, columns], r_sems.at[g, n])
        total = tokens[:, columns].astype(F32) + part[pl.ds(own_rows, 64), columns].astype(F32)
        for n in range(len(others)):
            total = total + landed[n, :, columns].astype(F32)
        result[:, columns] = total.astype(BF16)

    for copy in started:
        copy.wait_send()


def on_device(tokens, norm_gain, in_weight, short_filter, long_filter, skip_gain, out_weight):
    depth, _, channels = in_weight.shape
    block = 512
    width = norm_gain.shape[0]
    chunked = in_weight.reshape(depth, 3, CHUNKS, LANES).transpose(2, 0, 1, 3).reshape(CHUNKS, depth, 3 * LANES)
    vmem = pl.BlockSpec(memory_space=pltpu.VMEM)
    hbm = pl.BlockSpec(memory_space=pl.ANY)
    return pl.pallas_call(
        kernel,
        out_shape=jax.ShapeDtypeStruct(tokens.shape, BF16),
        in_specs=[vmem, vmem, hbm, vmem, vmem, vmem, hbm],
        out_specs=vmem,
        scratch_shapes=[
            pltpu.VMEM((block, width), BF16),
            pltpu.VMEM((CHUNKS, width, 3 * LANES), BF16),
            pltpu.VMEM((16, channels, 256), BF16),
            pltpu.VMEM((CHUNKS, HALO + block, 3 * LANES), BF16),
            pltpu.VMEM((3, HALO + block, LANES), F32),
            pltpu.VMEM((block, LANES), F32),
            pltpu.VMEM((block + 128, LANES), F32),
            pltpu.VMEM((block, channels), BF16),
            pltpu.VMEM((block, width), BF16),
            pltpu.VMEM((7, 64, width), BF16),
            pltpu.SemaphoreType.DMA((180,)),
            pltpu.SemaphoreType.DMA((CHUNKS + 1, 4, 2, 3)),
            pltpu.SemaphoreType.DMA((2, 4, 2)),
            pltpu.SemaphoreType.DMA((CHUNKS,)),
            pltpu.SemaphoreType.DMA((8, 7)),
            pltpu.SemaphoreType.DMA((CHUNKS + 1,)),
        ],
        compiler_params=pltpu.CompilerParams(
            collective_id=0, has_side_effects=True, vmem_limit_bytes=58 * 2**20
        ),
        cost_estimate=pl.CostEstimate(flops=9_000_000_000, bytes_accessed=4_000_000, transcendentals=64),
    )(
        tokens,
        norm_gain.reshape(1, width),
        chunked,
        short_filter,
        long_filter,
        skip_gain.reshape(1, channels),
        out_weight,
    )


def solution(mesh):
    placed = (
        P(("seq", "tp"), None),
        P(),
        P("seq", None, "tp"),
        P(None, None, "tp"),
        P(None, "tp"),
        P("tp"),
        P("tp", "seq"),
    )
    return jax.shard_map(
        on_device, mesh=mesh, in_specs=placed, out_specs=P(("seq", "tp"), None), check_vma=False
    )
```

```python
import functools

import jax
import jax.numpy as jnp
from jax import lax
from jax.experimental import pallas as pl
from jax.experimental.pallas import tpu as pltpu
from jax.sharding import PartitionSpec as P

MESH = pl.DeviceIdType.MESH
BF16 = jnp.bfloat16
F32 = jnp.float32

CHUNKS = 4
LANES = 128
HALO = 144
Z_FIRST = (1,)
RS_X_FIRST = (1, 3, 5, 7)


def in_proj(normed, weights, wide, halo, k, half):
    rows = normed.shape[0] // 2
    slot = k % 2
    at = pl.multiple_of(half * rows, rows)
    out = jnp.dot(normed[pl.ds(at, rows), :], weights[k], preferred_element_type=F32).astype(BF16)
    for p in range(3):
        wide[slot, p, pl.ds(pl.multiple_of(HALO + at, 8), rows), :] = out[:, p * LANES : (p + 1) * LANES].astype(F32)

    @pl.when(half == 1)
    def _():
        halo[k, 0] = out[rows - HALO :]


def featurize(short_ref, halo, wide, query, gate, k, first_block):
    block = query.shape[1]
    slot = k % 2
    keep = jnp.where(first_block, 0.0, 1.0).astype(F32)
    for p in range(3):
        wide[slot, p, 0:HALO, :] = halo[k, 1, :, p * LANES : (p + 1) * LANES].astype(F32) * keep
    taps = [[short_ref[p, j : j + 1, k * LANES : (k + 1) * LANES] for j in range(7)] for p in range(3)]

    def filt(p, first, rows):
        out = taps[p][0] * wide[slot, p, pl.ds(first, rows), :]
        for j in range(1, 7):
            out = out + taps[p][j] * wide[slot, p, pl.ds(first - j, rows), :]
        return out

    def gates(i, carry):
        at = pl.multiple_of(i * 64, 64)
        value = filt(1, 16 + at, 64) * filt(2, 16 + at, 64)
        gate[k, pl.ds(at, 64), :] = value.astype(BF16).astype(F32)
        return carry

    lax.fori_loop(0, (block + 128) // 64, gates, 0)

    def queries(i, carry):
        at = pl.multiple_of(i * 64, 64)
        query[k, pl.ds(at, 64), :] = filt(0, HALO + at, 64)
        return carry

    lax.fori_loop(0, block // 64, queries, 0)


def long_conv(gate, query, long_ref, skip_ref, mixed, k, half):
    columns = slice(k * LANES, (k + 1) * LANES)
    rows = query.shape[1] // 2
    tile = 128

    def body(i, carry):
        at = pl.multiple_of(half * rows + i * tile, tile)

        def eight_taps(group, total):
            first = pl.multiple_of(group * 8, 8)
            taps = long_ref[pl.ds(first, 8), columns]
            for b in range(8):
                total = total + taps[b : b + 1] * gate[k, pl.ds(128 + at - first - b, tile), :]
            return total

        total = skip_ref[:, columns] * gate[k, pl.ds(128 + at, tile), :]
        total = lax.fori_loop(0, long_ref.shape[0] // 8, eight_taps, total)
        mixed[pl.ds(at, tile), columns] = (query[k, pl.ds(at, tile), :] * total).astype(BF16)
        return carry

    lax.fori_loop(0, rows // tile, body, 0)


def kernel(
    tokens,
    gain,
    in_w,
    short_ref,
    long_ref,
    skip_ref,
    out_w,
    result,
    normed,
    weights,
    out_weights,
    halo,
    wide,
    query,
    gate,
    mixed,
    part,
    over_x,
    over_y,
    send_sems,
    w_sems,
    t_sems,
    h_sems,
    r_sems,
    l_sems,
):
    s, t = lax.axis_index("seq"), lax.axis_index("tp")
    z, xl, core = s // 4, (s // 2) % 2, s % 2
    xh, y = t // 4, t % 4

    def on_seq(dz, dx, dc):
        return ((z + dz) % 4) * 4 + ((xl + dx) % 2) * 2 + (core + dc) % 2

    def on_tp(dx, dy):
        return ((xh + dx) % 2) * 4 + (y + dy) % 4

    def seq_device(dz, dx, dc):
        return (on_seq(dz, dx, dc), t)

    def tp_device(dx, dy):
        return (s, on_tp(dx, dy))

    after = (lax.rem(s + 1, 16), t)
    before = (lax.rem(s + 15, 16), t)
    sibling = seq_device(0, 0, 1)

    partners = [sibling, seq_device(0, 1, 0), seq_device(1, 0, 0), seq_device(3, 0, 0), after, before]
    partners += [tp_device(dx, dy) for dx in range(2) for dy in range(4) if dx or dy]
    barrier = pltpu.get_barrier_semaphore()
    for partner in partners:
        pl.semaphore_signal(barrier, inc=1, device_id=partner, device_id_type=MESH)

    started, loaded = [], []

    def send(src, dst, recv_sem, device):
        copy = pltpu.make_async_remote_copy(
            src_ref=src,
            dst_ref=dst,
            send_sem=send_sems.at[len(started)],
            recv_sem=recv_sem,
            device_id=device,
            device_id_type=MESH,
        )
        copy.start()
        started.append(copy)

    def arrived(dst, recv_sem):
        pltpu.make_async_remote_copy(
            src_ref=dst,
            dst_ref=dst,
            send_sem=send_sems.at[0],
            recv_sem=recv_sem,
            device_id=sibling,
            device_id_type=MESH,
        ).wait_recv()

    local = []
    for k in range(CHUNKS):
        rows = weights.at[k, pl.ds(pl.multiple_of(s * 256, 256), 256)]
        local.append(
            [
                pltpu.make_async_copy(
                    in_w.at[p, :, pl.ds(k * LANES, LANES)], rows.at[:, pl.ds(p * LANES, LANES)], l_sems.at[k, p]
                )
                for p in range(3)
            ]
        )
    local.append([pltpu.make_async_copy(out_w, out_weights.at[s], l_sems.at[CHUNKS, 0])])
    for copies in local:
        for copy in copies:
            copy.start()

    own_rows = pl.multiple_of(t * 64, 64)
    for i in range(4):
        rows = tokens[i * 16 : (i + 1) * 16, :].astype(F32)
        scale = lax.rsqrt(jnp.mean(rows * rows, axis=-1, keepdims=True) + 1e-06)
        normed[pl.ds(own_rows + i * 16, 16), :] = (rows * scale * gain[...]).astype(BF16)

    pl.semaphore_wait(barrier, len(partners))

    def token_rows(dx, dy, half=None):
        first = on_tp(dx, dy) * 64
        if half is None:
            return normed.at[pl.ds(pl.multiple_of(first, 64), 64)]
        return normed.at[pl.ds(pl.multiple_of(first + 32 * half, 32), 32)]

    def t_round(dx):
        rows = token_rows(dx, 0)
        send(rows, rows, t_sems.at[dx, 3, 0], tp_device(0, 1))
        send(rows, rows, t_sems.at[dx, 1, 0], tp_device(0, 3))

    def t_start():
        send(token_rows(0, 0), token_rows(0, 0), t_sems.at[1, 0, 0], tp_device(1, 0))
        t_round(0)

    def t_cross():
        arrived(token_rows(1, 0), t_sems.at[1, 0, 0])
        t_round(1)

    def t_pass(dx, dy):
        arrived(token_rows(dx, dy), t_sems.at[dx, dy, 0])
        half = 0 if dy == 3 else 1
        rows = token_rows(dx, dy, half)
        send(rows, rows, t_sems.at[dx, 2, half], tp_device(0, 4 - dy))

    def t_last(dx):
        for half in range(2):
            arrived(token_rows(dx, 2, half), t_sems.at[dx, 2, half])

    def shard(k, dz, dx, dc=0, half=None):
        origin = on_seq(dz, dx, dc)
        if k < CHUNKS:
            ref, depth = weights.at[k], 256
            first = origin * 256
        else:
            ref, depth = out_weights.at[origin], 512
            first = 0
        if half is None:
            return ref.at[pl.ds(pl.multiple_of(first, 256), depth)]
        return ref.at[pl.ds(pl.multiple_of(first + half * (depth // 2), 128), depth // 2)]

    def w_send(k, dz, dx, device, slot_dz, slot_dx, index=0, half=None):
        ref = shard(k, dz, dx, 0, half)
        send(ref, ref, w_sems.at[k, slot_dz, slot_dx, index], device)

    def w_arrived(k, dz, dx):
        if dz == 2 and (dx == 0 or k not in Z_FIRST):
            for half in range(2):
                arrived(shard(k, dz, dx, 0, half), w_sems.at[k, dz, dx, half])
        else:
            arrived(shard(k, dz, dx), w_sems.at[k, dz, dx, 0])

    def w_sibling(k, dz, dx):
        w_send(k, dz, dx, sibling, dz, dx, 2)

    def w_along_x(k, dz):
        w_send(k, dz, 0, seq_device(0, 1, 0), dz, 1)

    def w_round(k, dx):
        w_send(k, 0, dx, seq_device(1, 0, 0), 3, dx)
        w_send(k, 0, dx, seq_device(3, 0, 0), 1, dx)

    def w_pass(k, dz, dx):
        half = 0 if dz == 3 else 1
        w_send(k, dz, dx, seq_device(4 - dz, 0, 0), 2, dx, half, half)

    def w_own_x(k):
        if k not in loaded:
            loaded.append(k)
            for copy in local[k]:
                copy.wait()
        w_along_x(k, 0)

    def w_own_z(k):
        if k not in loaded:
            loaded.append(k)
            for copy in local[k]:
                copy.wait()
        w_round(k, 0)

    def w_x(k):
        w_arrived(k, 0, 1)
        w_round(k, 1)
        w_sibling(k, 0, 1)

    def w_z(k, dz):
        w_arrived(k, dz, 0)
        w_pass(k, dz, 0)
        if k in Z_FIRST:
            w_along_x(k, dz)
        w_sibling(k, dz, 0)

    def w_turn(k, dz):
        w_arrived(k, dz, 1)
        w_pass(k, dz, 1)
        w_sibling(k, dz, 1)

    def w_far(k, dx):
        w_arrived(k, 2, dx)
        if k in Z_FIRST:
            w_along_x(k, 2)
        w_sibling(k, 2, dx)

    def w_end(k, dz):
        w_arrived(k, dz, 1)
        w_sibling(k, dz, 1)

    def w_from_sibling(k, dz, dx):
        arrived(shard(k, dz, dx, 1), w_sems.at[k, dz, dx, 2])

    def w_ready(k):
        for dz in range(4):
            for dx in range(2):
                w_from_sibling(k, dz, dx)

    def half_of(side):
        return (xh + side) % 2

    def project(k, side):
        in_proj(normed, weights, wide, halo, k, half_of(side))

    def halo_send(k):
        send(halo.at[k, 0], halo.at[k, 1], h_sems.at[k], after)

    def feature(k):
        arrived(halo.at[k, 1], h_sems.at[k])
        featurize(short_ref, halo, wide, query, gate, k, s == 0)

    def conv(k, side):
        long_conv(gate, query, long_ref, skip_ref, mixed, k, half_of(side))

    groups = [(0, 0), (0, 1), (3, 0), (1, 0), (3, 1), (1, 1), (2, 0), (2, 1)]
    round_y = (2, 1, 3)

    def columns_of(g):
        return pl.ds(pl.multiple_of(on_seq(*groups[g], 0) // 2 * 512, 512), 512)

    def y_rows(dy):
        return pl.ds(pl.multiple_of((y + dy) % 4 * 64, 64), 64)

    def project_out(g, side):
        first = on_seq(*groups[g], 0) // 2 * 2
        half = half_of(side)

        def body(i, carry):
            origin = first + i
            rows = mixed[pl.ds(pl.multiple_of(half * 256, 256), 256), :]
            out = jnp.dot(rows, out_weights[origin], preferred_element_type=F32)
            part[half, :, pl.ds(pl.multiple_of(origin * 256, 256), 256)] = out.astype(BF16)
            return carry

        lax.fori_loop(0, 2, body, 0)

    def round_send(g, side, stage, slot):
        for dy in round_y:
            send(
                part.at[half_of(side), y_rows(dy), columns_of(g)],
                over_y.at[g, dy - 1, slot],
                r_sems.at[g, stage, dy - 1],
                tp_device(0, dy),
            )

    def round_arrived(g, stage, slot):
        for dy in round_y:
            arrived(over_y.at[g, dy - 1, slot], r_sems.at[g, stage, dy - 1])

    def emit(g, side):
        if side == 1:
            w_from_sibling(CHUNKS, *groups[g])
        project_out(g, side)
        if g not in RS_X_FIRST:
            round_send(g, side, 0 if side == 1 else 2, side)
        elif side == 1:
            send(part.at[half_of(1), :, columns_of(g)], over_x.at[g], r_sems.at[g, 0, 0], tp_device(1, 0))

    def stage_two(g):
        cols = columns_of(g)
        if g in RS_X_FIRST:
            arrived(over_x.at[g], r_sems.at[g, 0, 0])

            def body(i, carry):
                rows = pl.ds(pl.multiple_of(i * 64, 64), 64)
                both = part[xh, rows, cols].astype(F32) + over_x[g, rows, :].astype(F32)
                part[xh, rows, cols] = both.astype(BF16)
                return carry

            lax.fori_loop(0, 4, body, 0)
            round_send(g, 0, 1, 0)
        else:
            round_arrived(g, 0, 1)
            theirs = part[1 - xh, y_rows(0), cols].astype(F32)
            for dy in round_y:
                theirs = theirs + over_y[g, dy - 1, 1].astype(F32)
            part[1 - xh, y_rows(0), cols] = theirs.astype(BF16)
            send(part.at[1 - xh, y_rows(0), cols], over_x.at[g, pl.ds(0, 64)], r_sems.at[g, 1, 0], tp_device(1, 0))

    def finish(g):
        cols = columns_of(g)
        total = tokens[:, cols].astype(F32) + part[xh, y_rows(0), cols].astype(F32)
        round_arrived(g, 1 if g in RS_X_FIRST else 2, 0)
        for dy in round_y:
            total = total + over_y[g, dy - 1, 0].astype(F32)
        if g not in RS_X_FIRST:
            arrived(over_x.at[g, pl.ds(0, 64)], r_sems.at[g, 1, 0])
            total = total + over_x[g, 0:64, :].astype(F32)
        result[:, cols] = total.astype(BF16)

    t_start()
    w_own_x(0)
    w_own_z(0)
    w_sibling(0, 0, 0)
    w_own_x(1)
    w_own_z(1)
    w_sibling(1, 0, 0)
    w_own_z(2)
    w_sibling(2, 0, 0)
    w_own_z(3)
    w_sibling(3, 0, 0)
    w_own_x(2)
    w_z(0, 3)
    w_z(0, 1)
    w_own_x(3)
    w_z(1, 3)
    w_z(1, 1)
    t_pass(0, 3)
    t_pass(0, 1)
    t_cross()
    w_z(2, 3)
    w_z(2, 1)
    w_x(0)
    w_z(3, 3)
    w_z(3, 1)
    t_last(0)
    w_far(0, 0)
    w_end(1, 0)
    w_far(1, 0)
    w_far(2, 0)
    w_x(2)
    w_turn(0, 3)
    w_turn(0, 1)
    w_x(3)
    t_pass(1, 3)
    t_pass(1, 1)
    w_far(3, 0)
    w_end(1, 3)
    w_turn(2, 3)
    w_turn(2, 1)
    w_own_x(4)
    w_far(0, 1)
    w_end(1, 1)
    t_last(1)
    w_own_z(4)
    w_sibling(4, 0, 0)
    w_ready(0)
    project(0, 0)
    project(0, 1)
    w_end(1, 2)
    w_turn(3, 1)
    w_turn(3, 3)
    halo_send(0)
    w_far(2, 1)
    w_ready(1)
    project(1, 0)
    feature(0)
    w_ready(2)
    project(1, 1)
    halo_send(1)
    w_x(4)
    project(2, 0)
    w_z(4, 1)
    w_z(4, 3)
    feature(1)
    project(2, 1)
    w_far(3, 1)
    halo_send(2)
    conv(0, 1)
    w_ready(3)
    feature(2)
    project(3, 0)
    project(3, 1)
    halo_send(3)
    w_turn(4, 1)
    w_turn(4, 3)
    conv(1, 1)
    feature(3)
    w_far(4, 0)
    conv(2, 1)
    conv(3, 1)
    w_far(4, 1)
    emit(0, 1)
    emit(1, 1)
    emit(2, 1)
    emit(3, 1)
    emit(4, 1)
    emit(5, 1)
    emit(6, 1)
    stage_two(0)
    emit(7, 1)
    conv(0, 0)
    stage_two(2)
    conv(1, 0)
    stage_two(4)
    conv(2, 0)
    stage_two(6)
    conv(3, 0)
    emit(0, 0)
    emit(1, 0)
    stage_two(1)
    emit(2, 0)
    emit(3, 0)
    stage_two(3)
    emit(4, 0)
    emit(5, 0)
    emit(6, 0)
    emit(7, 0)
    finish(1)
    stage_two(5)
    finish(0)
    finish(3)
    stage_two(7)
    finish(2)
    finish(5)
    finish(4)
    finish(6)
    finish(7)
    for copy in started:
        copy.wait_send()


def on_device(tokens, norm_gain, in_weight, short_filter, long_filter, skip_gain, out_weight):
    channels = in_weight.shape[2]
    block = 512
    width = norm_gain.shape[0]
    vmem = pl.BlockSpec(memory_space=pltpu.VMEM)
    hbm = pl.BlockSpec(memory_space=pl.ANY)
    return pl.pallas_call(
        kernel,
        out_shape=jax.ShapeDtypeStruct(tokens.shape, BF16),
        in_specs=[vmem, vmem, hbm, vmem, vmem, vmem, hbm],
        out_specs=vmem,
        scratch_shapes=[
            pltpu.VMEM((block, width), BF16),
            pltpu.VMEM((CHUNKS, width, 3 * LANES), BF16),
            pltpu.VMEM((16, channels, 256), BF16),
            pltpu.VMEM((CHUNKS, 2, HALO, 3 * LANES), BF16),
            pltpu.VMEM((2, 3, HALO + block, LANES), F32),
            pltpu.VMEM((CHUNKS, block, LANES), F32),
            pltpu.VMEM((CHUNKS, block + 128, LANES), F32),
            pltpu.VMEM((block, channels), BF16),
            pltpu.VMEM((2, block // 2, width), BF16),
            pltpu.VMEM((8, block // 2, 512), BF16),
            pltpu.VMEM((8, 3, 2, 64, 512), BF16),
            pltpu.SemaphoreType.DMA((180,)),
            pltpu.SemaphoreType.DMA((CHUNKS + 1, 4, 2, 3)),
            pltpu.SemaphoreType.DMA((2, 4, 2)),
            pltpu.SemaphoreType.DMA((CHUNKS,)),
            pltpu.SemaphoreType.DMA((8, 3, 3)),
            pltpu.SemaphoreType.DMA((CHUNKS + 1, 3)),
        ],
        compiler_params=pltpu.CompilerParams(
            collective_id=0, has_side_effects=True, vmem_limit_bytes=58 * 2**20
        ),
        cost_estimate=pl.CostEstimate(flops=9_000_000_000, bytes_accessed=4_000_000, transcendentals=64),
    )(
        tokens,
        norm_gain.reshape(1, width),
        in_weight.transpose(1, 0, 2),
        short_filter.transpose(1, 0, 2),
        long_filter,
        skip_gain.reshape(1, channels),
        out_weight,
    )


def solution(mesh):
    placed = (
        P(("seq", "tp"), None),
        P(),
        P("seq", None, "tp"),
        P(None, None, "tp"),
        P(None, "tp"),
        P("tp"),
        P("tp", "seq"),
    )
    return jax.shard_map(
        on_device, mesh=mesh, in_specs=placed, out_specs=P(("seq", "tp"), None), check_vma=False
    )
```

```python
import functools

import jax
import jax.numpy as jnp
from jax import lax
from jax.experimental import pallas as pl
from jax.experimental.pallas import tpu as pltpu
from jax.sharding import PartitionSpec as P

MESH = pl.DeviceIdType.MESH
BF16 = jnp.bfloat16
F32 = jnp.float32

CHUNKS = 4
LANES = 128
HALO = 144
Z_FIRST = (2,)
RS_X_FIRST = (1, 3, 5, 7)


def in_proj(normed, weights, wide, halo, k, half):
    rows = normed.shape[0] // 2
    slot = k % 2
    at = pl.multiple_of(half * rows, rows)
    out = jnp.dot(normed[pl.ds(at, rows), :], weights[k], preferred_element_type=F32).astype(BF16)
    for p in range(3):
        wide[slot, p, pl.ds(pl.multiple_of(HALO + at, 8), rows), :] = out[:, p * LANES : (p + 1) * LANES].astype(F32)

    @pl.when(half == 1)
    def _():
        halo[k, 0] = out[rows - HALO :]


def featurize(short_ref, halo, wide, query, gate, k, first_block):
    block = query.shape[1]
    slot = k % 2
    keep = jnp.where(first_block, 0.0, 1.0).astype(F32)
    for p in range(3):
        wide[slot, p, 0:HALO, :] = halo[k, 1, :, p * LANES : (p + 1) * LANES].astype(F32) * keep
    taps = [[short_ref[p, j : j + 1, k * LANES : (k + 1) * LANES] for j in range(7)] for p in range(3)]

    def filt(p, first, rows):
        out = taps[p][0] * wide[slot, p, pl.ds(first, rows), :]
        for j in range(1, 7):
            out = out + taps[p][j] * wide[slot, p, pl.ds(first - j, rows), :]
        return out

    def gates(i, carry):
        at = pl.multiple_of(i * 64, 64)
        value = filt(1, 16 + at, 64) * filt(2, 16 + at, 64)
        gate[k, pl.ds(at, 64), :] = value.astype(BF16).astype(F32)
        return carry

    lax.fori_loop(0, (block + 128) // 64, gates, 0)

    def queries(i, carry):
        at = pl.multiple_of(i * 64, 64)
        query[k, pl.ds(at, 64), :] = filt(0, HALO + at, 64)
        return carry

    lax.fori_loop(0, block // 64, queries, 0)


def long_conv(gate, query, long_ref, skip_ref, mixed, k, half):
    columns = slice(k * LANES, (k + 1) * LANES)
    rows = query.shape[1] // 2
    tile = 128

    def body(i, carry):
        at = pl.multiple_of(half * rows + i * tile, tile)

        def eight_taps(group, total):
            first = pl.multiple_of(group * 8, 8)
            taps = long_ref[pl.ds(first, 8), columns]
            for b in range(8):
                total = total + taps[b : b + 1] * gate[k, pl.ds(128 + at - first - b, tile), :]
            return total

        total = skip_ref[:, columns] * gate[k, pl.ds(128 + at, tile), :]
        total = lax.fori_loop(0, long_ref.shape[0] // 8, eight_taps, total)
        mixed[pl.ds(at, tile), columns] = (query[k, pl.ds(at, tile), :] * total).astype(BF16)
        return carry

    lax.fori_loop(0, rows // tile, body, 0)


def kernel(
    tokens,
    gain,
    in_w,
    short_ref,
    long_ref,
    skip_ref,
    out_w,
    result,
    normed,
    weights,
    out_weights,
    halo,
    wide,
    query,
    gate,
    mixed,
    part,
    over_x,
    over_y,
    send_sems,
    w_sems,
    t_sems,
    h_sems,
    r_sems,
    l_sems,
):
    s, t = lax.axis_index("seq"), lax.axis_index("tp")
    z, xl, core = s // 4, (s // 2) % 2, s % 2
    xh, y = t // 4, t % 4

    def on_seq(dz, dx, dc):
        return ((z + dz) % 4) * 4 + ((xl + dx) % 2) * 2 + (core + dc) % 2

    def on_tp(dx, dy):
        return ((xh + dx) % 2) * 4 + (y + dy) % 4

    def seq_device(dz, dx, dc):
        return (on_seq(dz, dx, dc), t)

    def tp_device(dx, dy):
        return (s, on_tp(dx, dy))

    after = (lax.rem(s + 1, 16), t)
    before = (lax.rem(s + 15, 16), t)
    sibling = seq_device(0, 0, 1)

    partners = [sibling, seq_device(0, 1, 0), seq_device(1, 0, 0), seq_device(3, 0, 0), after, before]
    partners += [tp_device(dx, dy) for dx in range(2) for dy in range(4) if dx or dy]
    barrier = pltpu.get_barrier_semaphore()
    for partner in partners:
        pl.semaphore_signal(barrier, inc=1, device_id=partner, device_id_type=MESH)

    started, loaded = [], []

    def send(src, dst, recv_sem, device):
        copy = pltpu.make_async_remote_copy(
            src_ref=src,
            dst_ref=dst,
            send_sem=send_sems.at[len(started)],
            recv_sem=recv_sem,
            device_id=device,
            device_id_type=MESH,
        )
        copy.start()
        started.append(copy)

    def arrived(dst, recv_sem):
        pltpu.make_async_remote_copy(
            src_ref=dst,
            dst_ref=dst,
            send_sem=send_sems.at[0],
            recv_sem=recv_sem,
            device_id=sibling,
            device_id_type=MESH,
        ).wait_recv()

    local = []
    for k in range(CHUNKS):
        rows = weights.at[k, pl.ds(pl.multiple_of(s * 256, 256), 256)]
        local.append(
            [
                pltpu.make_async_copy(
                    in_w.at[p, :, pl.ds(k * LANES, LANES)], rows.at[:, pl.ds(p * LANES, LANES)], l_sems.at[k, p]
                )
                for p in range(3)
            ]
        )
    local.append([pltpu.make_async_copy(out_w, out_weights.at[s], l_sems.at[CHUNKS, 0])])
    for copies in local:
        for copy in copies:
            copy.start()

    own_rows = pl.multiple_of(t * 64, 64)
    for i in range(4):
        rows = tokens[i * 16 : (i + 1) * 16, :].astype(F32)
        scale = lax.rsqrt(jnp.mean(rows * rows, axis=-1, keepdims=True) + 1e-06)
        normed[pl.ds(own_rows + i * 16, 16), :] = (rows * scale * gain[...]).astype(BF16)

    pl.semaphore_wait(barrier, len(partners))

    def token_rows(dx, dy, half=None):
        first = on_tp(dx, dy) * 64
        if half is None:
            return normed.at[pl.ds(pl.multiple_of(first, 64), 64)]
        return normed.at[pl.ds(pl.multiple_of(first + 32 * half, 32), 32)]

    def t_round(dx):
        rows = token_rows(dx, 0)
        send(rows, rows, t_sems.at[dx, 3, 0], tp_device(0, 1))
        send(rows, rows, t_sems.at[dx, 1, 0], tp_device(0, 3))

    def t_start():
        send(token_rows(0, 0), token_rows(0, 0), t_sems.at[1, 0, 0], tp_device(1, 0))
        t_round(0)

    def t_cross():
        arrived(token_rows(1, 0), t_sems.at[1, 0, 0])
        t_round(1)

    def t_pass(dx, dy):
        arrived(token_rows(dx, dy), t_sems.at[dx, dy, 0])
        half = 0 if dy == 3 else 1
        rows = token_rows(dx, dy, half)
        send(rows, rows, t_sems.at[dx, 2, half], tp_device(0, 4 - dy))

    def t_last(dx):
        for half in range(2):
            arrived(token_rows(dx, 2, half), t_sems.at[dx, 2, half])

    def shard(k, dz, dx, dc=0, half=None):
        origin = on_seq(dz, dx, dc)
        if k < CHUNKS:
            ref, depth = weights.at[k], 256
            first = origin * 256
        else:
            ref, depth = out_weights.at[origin], 512
            first = 0
        if half is None:
            return ref.at[pl.ds(pl.multiple_of(first, 256), depth)]
        return ref.at[pl.ds(pl.multiple_of(first + half * (depth // 2), 128), depth // 2)]

    def w_send(k, dz, dx, device, slot_dz, slot_dx, index=0, half=None):
        ref = shard(k, dz, dx, 0, half)
        send(ref, ref, w_sems.at[k, slot_dz, slot_dx, index], device)

    def w_arrived(k, dz, dx):
        if dz == 2 and (dx == 0 or k not in Z_FIRST):
            for half in range(2):
                arrived(shard(k, dz, dx, 0, half), w_sems.at[k, dz, dx, half])
        else:
            arrived(shard(k, dz, dx), w_sems.at[k, dz, dx, 0])

    def w_sibling(k, dz, dx):
        w_send(k, dz, dx, sibling, dz, dx, 2)

    def w_along_x(k, dz):
        w_send(k, dz, 0, seq_device(0, 1, 0), dz, 1)

    def w_round(k, dx):
        w_send(k, 0, dx, seq_device(1, 0, 0), 3, dx)
        w_send(k, 0, dx, seq_device(3, 0, 0), 1, dx)

    def w_pass(k, dz, dx):
        half = 0 if dz == 3 else 1
        w_send(k, dz, dx, seq_device(4 - dz, 0, 0), 2, dx, half, half)

    def w_own_x(k):
        if k not in loaded:
            loaded.append(k)
            for copy in local[k]:
                copy.wait()
        w_along_x(k, 0)

    def w_own_z(k):
        if k not in loaded:
            loaded.append(k)
            for copy in local[k]:
                copy.wait()
        w_round(k, 0)

    def w_x(k):
        w_arrived(k, 0, 1)
        w_round(k, 1)
        w_sibling(k, 0, 1)

    def w_z(k, dz):
        w_arrived(k, dz, 0)
        w_pass(k, dz, 0)
        if k in Z_FIRST:
            w_along_x(k, dz)
        w_sibling(k, dz, 0)

    def w_turn(k, dz):
        w_arrived(k, dz, 1)
        w_pass(k, dz, 1)
        w_sibling(k, dz, 1)

    def w_far(k, dx):
        w_arrived(k, 2, dx)
        if k in Z_FIRST:
            w_along_x(k, 2)
        w_sibling(k, 2, dx)

    def w_end(k, dz):
        w_arrived(k, dz, 1)
        w_sibling(k, dz, 1)

    def w_from_sibling(k, dz, dx):
        arrived(shard(k, dz, dx, 1), w_sems.at[k, dz, dx, 2])

    def w_ready(k):
        for dz in range(4):
            for dx in range(2):
                w_from_sibling(k, dz, dx)

    def half_of(side):
        return (xh + side) % 2

    def project(k, side):
        in_proj(normed, weights, wide, halo, k, half_of(side))

    def halo_send(k):
        send(halo.at[k, 0], halo.at[k, 1], h_sems.at[k], after)

    def feature(k):
        arrived(halo.at[k, 1], h_sems.at[k])
        featurize(short_ref, halo, wide, query, gate, k, s == 0)

    def conv(k, side):
        long_conv(gate, query, long_ref, skip_ref, mixed, k, half_of(side))

    groups = [(0, 0), (0, 1), (3, 0), (1, 0), (3, 1), (1, 1), (2, 0), (2, 1)]
    round_y = (2, 1, 3)

    def columns_of(g):
        return pl.ds(pl.multiple_of(on_seq(*groups[g], 0) // 2 * 512, 512), 512)

    def y_rows(dy):
        return pl.ds(pl.multiple_of((y + dy) % 4 * 64, 64), 64)

    def project_out(g, side):
        first = on_seq(*groups[g], 0) // 2 * 2
        half = half_of(side)

        def body(i, carry):
            origin = first + i
            rows = mixed[pl.ds(pl.multiple_of(half * 256, 256), 256), :]
            out = jnp.dot(rows, out_weights[origin], preferred_element_type=F32)
            part[half, :, pl.ds(pl.multiple_of(origin * 256, 256), 256)] = out.astype(BF16)
            return carry

        lax.fori_loop(0, 2, body, 0)

    def round_send(g, side, stage, slot):
        for dy in round_y:
            send(
                part.at[half_of(side), y_rows(dy), columns_of(g)],
                over_y.at[g, dy - 1, slot],
                r_sems.at[g, stage, dy - 1],
                tp_device(0, dy),
            )

    def round_arrived(g, stage, slot):
        for dy in round_y:
            arrived(over_y.at[g, dy - 1, slot], r_sems.at[g, stage, dy - 1])

    def emit(g, side):
        if side == 1:
            w_from_sibling(CHUNKS, *groups[g])
        project_out(g, side)
        if g not in RS_X_FIRST:
            round_send(g, side, 0 if side == 1 else 2, side)
        elif side == 1:
            send(part.at[half_of(1), :, columns_of(g)], over_x.at[g], r_sems.at[g, 0, 0], tp_device(1, 0))

    def stage_two(g):
        cols = columns_of(g)
        if g in RS_X_FIRST:
            arrived(over_x.at[g], r_sems.at[g, 0, 0])

            def body(i, carry):
                rows = pl.ds(pl.multiple_of(i * 64, 64), 64)
                both = part[xh, rows, cols].astype(F32) + over_x[g, rows, :].astype(F32)
                part[xh, rows, cols] = both.astype(BF16)
                return carry

            lax.fori_loop(0, 4, body, 0)
            round_send(g, 0, 1, 0)
        else:
            round_arrived(g, 0, 1)
            theirs = part[1 - xh, y_rows(0), cols].astype(F32)
            for dy in round_y:
                theirs = theirs + over_y[g, dy - 1, 1].astype(F32)
            part[1 - xh, y_rows(0), cols] = theirs.astype(BF16)
            send(part.at[1 - xh, y_rows(0), cols], over_x.at[g, pl.ds(0, 64)], r_sems.at[g, 1, 0], tp_device(1, 0))

    def finish(g):
        cols = columns_of(g)
        total = tokens[:, cols].astype(F32) + part[xh, y_rows(0), cols].astype(F32)
        round_arrived(g, 1 if g in RS_X_FIRST else 2, 0)
        for dy in round_y:
            total = total + over_y[g, dy - 1, 0].astype(F32)
        if g not in RS_X_FIRST:
            arrived(over_x.at[g, pl.ds(0, 64)], r_sems.at[g, 1, 0])
            total = total + over_x[g, 0:64, :].astype(F32)
        result[:, cols] = total.astype(BF16)

    t_start()
    w_own_z(0)
    w_sibling(0, 0, 0)
    w_own_z(1)
    w_sibling(1, 0, 0)
    w_own_z(2)
    w_sibling(2, 0, 0)
    w_own_z(3)
    w_sibling(3, 0, 0)
    w_own_x(0)
    w_z(0, 3)
    w_z(0, 1)
    w_own_x(1)
    w_z(1, 3)
    w_z(1, 1)
    w_own_x(2)
    t_pass(0, 3)
    t_pass(0, 1)
    t_cross()
    w_z(2, 3)
    w_z(2, 1)
    w_x(0)
    w_z(3, 3)
    w_z(3, 1)
    w_far(0, 0)
    t_last(0)
    w_x(1)
    w_far(1, 0)
    w_own_x(3)
    w_own_x(4)
    w_far(2, 0)
    w_end(2, 0)
    w_turn(0, 3)
    w_turn(0, 1)
    w_end(2, 3)
    w_far(3, 0)
    t_pass(1, 3)
    t_pass(1, 1)
    w_end(2, 1)
    w_turn(1, 3)
    w_turn(1, 1)
    w_far(0, 1)
    w_x(3)
    w_own_z(4)
    w_sibling(4, 0, 0)
    w_far(1, 1)
    w_ready(0)
    t_last(1)
    project(0, 0)
    project(0, 1)
    halo_send(0)
    w_ready(1)
    project(1, 1)
    w_turn(3, 3)
    w_turn(3, 1)
    project(1, 0)
    halo_send(1)
    feature(0)
    w_x(4)
    conv(0, 1)
    feature(1)
    conv(1, 1)
    w_end(2, 2)
    conv(0, 0)
    w_z(4, 3)
    w_z(4, 1)
    conv(1, 0)
    w_far(3, 1)
    w_ready(2)
    project(2, 0)
    project(2, 1)
    halo_send(2)
    w_ready(3)
    project(3, 0)
    project(3, 1)
    halo_send(3)
    feature(2)
    conv(2, 1)
    feature(3)
    conv(3, 1)
    emit(0, 1)
    emit(1, 1)
    w_turn(4, 3)
    w_turn(4, 1)
    emit(2, 1)
    emit(3, 1)
    conv(2, 0)
    conv(3, 0)
    emit(0, 0)
    emit(1, 0)
    emit(2, 0)
    emit(3, 0)
    stage_two(0)
    w_far(4, 0)
    w_far(4, 1)
    stage_two(1)
    emit(4, 1)
    emit(5, 1)
    emit(4, 0)
    emit(5, 0)
    stage_two(2)
    stage_two(3)
    emit(6, 1)
    emit(7, 1)
    emit(6, 0)
    emit(7, 0)
    finish(0)
    stage_two(4)
    stage_two(5)
    finish(1)
    finish(2)
    finish(3)
    stage_two(6)
    stage_two(7)
    finish(4)
    finish(5)
    finish(6)
    finish(7)
    for copy in started:
        copy.wait_send()


def on_device(tokens, norm_gain, in_weight, short_filter, long_filter, skip_gain, out_weight):
    channels = in_weight.shape[2]
    block = 512
    width = norm_gain.shape[0]
    vmem = pl.BlockSpec(memory_space=pltpu.VMEM)
    hbm = pl.BlockSpec(memory_space=pl.ANY)
    return pl.pallas_call(
        kernel,
        out_shape=jax.ShapeDtypeStruct(tokens.shape, BF16),
        in_specs=[vmem, vmem, hbm, vmem, vmem, vmem, hbm],
        out_specs=vmem,
        scratch_shapes=[
            pltpu.VMEM((block, width), BF16),
            pltpu.VMEM((CHUNKS, width, 3 * LANES), BF16),
            pltpu.VMEM((16, channels, 256), BF16),
            pltpu.VMEM((CHUNKS, 2, HALO, 3 * LANES), BF16),
            pltpu.VMEM((2, 3, HALO + block, LANES), F32),
            pltpu.VMEM((CHUNKS, block, LANES), F32),
            pltpu.VMEM((CHUNKS, block + 128, LANES), F32),
            pltpu.VMEM((block, channels), BF16),
            pltpu.VMEM((2, block // 2, width), BF16),
            pltpu.VMEM((8, block // 2, 512), BF16),
            pltpu.VMEM((8, 3, 2, 64, 512), BF16),
            pltpu.SemaphoreType.DMA((180,)),
            pltpu.SemaphoreType.DMA((CHUNKS + 1, 4, 2, 3)),
            pltpu.SemaphoreType.DMA((2, 4, 2)),
            pltpu.SemaphoreType.DMA((CHUNKS,)),
            pltpu.SemaphoreType.DMA((8, 3, 3)),
            pltpu.SemaphoreType.DMA((CHUNKS + 1, 3)),
        ],
        compiler_params=pltpu.CompilerParams(
            collective_id=0, has_side_effects=True, vmem_limit_bytes=58 * 2**20
        ),
        cost_estimate=pl.CostEstimate(flops=9_000_000_000, bytes_accessed=4_000_000, transcendentals=64),
    )(
        tokens,
        norm_gain.reshape(1, width),
        in_weight.transpose(1, 0, 2),
        short_filter.transpose(1, 0, 2),
        long_filter,
        skip_gain.reshape(1, channels),
        out_weight,
    )


def solution(mesh):
    placed = (
        P(("seq", "tp"), None),
        P(),
        P("seq", None, "tp"),
        P(None, None, "tp"),
        P(None, "tp"),
        P("tp"),
        P("tp", "seq"),
    )
    return jax.shard_map(
        on_device, mesh=mesh, in_specs=placed, out_specs=P(("seq", "tp"), None), check_vma=False
    )
```

```python
import functools

import jax
import jax.numpy as jnp
from jax import lax
from jax.experimental import pallas as pl
from jax.experimental.pallas import tpu as pltpu
from jax.sharding import PartitionSpec as P

MESH = pl.DeviceIdType.MESH
BF16 = jnp.bfloat16
F32 = jnp.float32

CHUNKS = 4
LANES = 128
HALO = 144
Z_FIRST = (2,)
RS_X_FIRST = (1, 3, 5, 7)


def in_proj(normed, weights, wide, halo, k, half):
    rows = normed.shape[0] // 2
    slot = k % 2
    at = pl.multiple_of(half * rows, rows)
    out = jnp.dot(normed[pl.ds(at, rows), :], weights[k], preferred_element_type=F32).astype(BF16)
    for p in range(3):
        wide[slot, p, pl.ds(pl.multiple_of(HALO + at, 8), rows), :] = out[:, p * LANES : (p + 1) * LANES].astype(F32)

    @pl.when(half == 1)
    def _():
        halo[k, 0] = out[rows - HALO :]


def featurize(short_ref, halo, wide, query, gate, k, first_block):
    block = query.shape[1]
    slot = k % 2
    keep = jnp.where(first_block, 0.0, 1.0).astype(F32)
    for p in range(3):
        wide[slot, p, 0:HALO, :] = halo[k, 1, :, p * LANES : (p + 1) * LANES].astype(F32) * keep
    taps = [[short_ref[p, j : j + 1, k * LANES : (k + 1) * LANES] for j in range(7)] for p in range(3)]

    def filt(p, first, rows):
        out = taps[p][0] * wide[slot, p, pl.ds(first, rows), :]
        for j in range(1, 7):
            out = out + taps[p][j] * wide[slot, p, pl.ds(first - j, rows), :]
        return out

    def gates(i, carry):
        at = pl.multiple_of(i * 64, 64)
        value = filt(1, 16 + at, 64) * filt(2, 16 + at, 64)
        gate[k, pl.ds(at, 64), :] = value.astype(BF16).astype(F32)
        return carry

    lax.fori_loop(0, (block + 128) // 64, gates, 0)

    def queries(i, carry):
        at = pl.multiple_of(i * 64, 64)
        query[k, pl.ds(at, 64), :] = filt(0, HALO + at, 64)
        return carry

    lax.fori_loop(0, block // 64, queries, 0)


def long_conv(gate, query, long_ref, skip_ref, mixed, k, half):
    columns = slice(k * LANES, (k + 1) * LANES)
    rows = query.shape[1] // 2
    tile = 128

    def body(i, carry):
        at = pl.multiple_of(half * rows + i * tile, tile)

        def eight_taps(group, total):
            first = pl.multiple_of(group * 8, 8)
            taps = long_ref[pl.ds(first, 8), columns]
            for b in range(8):
                total = total + taps[b : b + 1] * gate[k, pl.ds(128 + at - first - b, tile), :]
            return total

        total = skip_ref[:, columns] * gate[k, pl.ds(128 + at, tile), :]
        total = lax.fori_loop(0, long_ref.shape[0] // 8, eight_taps, total)
        mixed[pl.ds(at, tile), columns] = (query[k, pl.ds(at, tile), :] * total).astype(BF16)
        return carry

    lax.fori_loop(0, rows // tile, body, 0)


def kernel(
    tokens,
    gain,
    in_w,
    short_ref,
    long_ref,
    skip_ref,
    out_w,
    result,
    normed,
    weights,
    out_weights,
    halo,
    wide,
    query,
    gate,
    mixed,
    part,
    over_x,
    over_y,
    send_sems,
    w_sems,
    t_sems,
    h_sems,
    r_sems,
    l_sems,
):
    s, t = lax.axis_index("seq"), lax.axis_index("tp")
    z, xl, core = s // 4, (s // 2) % 2, s % 2
    xh, y = t // 4, t % 4

    def on_seq(dz, dx, dc):
        return ((z + dz) % 4) * 4 + ((xl + dx) % 2) * 2 + (core + dc) % 2

    def on_tp(dx, dy):
        return ((xh + dx) % 2) * 4 + (y + dy) % 4

    def seq_device(dz, dx, dc):
        return (on_seq(dz, dx, dc), t)

    def tp_device(dx, dy):
        return (s, on_tp(dx, dy))

    after = (lax.rem(s + 1, 16), t)
    before = (lax.rem(s + 15, 16), t)
    sibling = seq_device(0, 0, 1)

    partners = [sibling, seq_device(0, 1, 0), seq_device(1, 0, 0), seq_device(3, 0, 0), after, before]
    partners += [tp_device(dx, dy) for dx in range(2) for dy in range(4) if dx or dy]
    barrier = pltpu.get_barrier_semaphore()
    for partner in partners:
        pl.semaphore_signal(barrier, inc=1, device_id=partner, device_id_type=MESH)

    started, loaded = [], []

    def send(src, dst, recv_sem, device):
        copy = pltpu.make_async_remote_copy(
            src_ref=src,
            dst_ref=dst,
            send_sem=send_sems.at[len(started)],
            recv_sem=recv_sem,
            device_id=device,
            device_id_type=MESH,
        )
        copy.start()
        started.append(copy)

    def arrived(dst, recv_sem):
        pltpu.make_async_remote_copy(
            src_ref=dst,
            dst_ref=dst,
            send_sem=send_sems.at[0],
            recv_sem=recv_sem,
            device_id=sibling,
            device_id_type=MESH,
        ).wait_recv()

    local = []
    for k in range(CHUNKS):
        rows = weights.at[k, pl.ds(pl.multiple_of(s * 256, 256), 256)]
        local.append(
            [
                pltpu.make_async_copy(
                    in_w.at[p, :, pl.ds(k * LANES, LANES)], rows.at[:, pl.ds(p * LANES, LANES)], l_sems.at[k, p]
                )
                for p in range(3)
            ]
        )
    local.append([pltpu.make_async_copy(out_w, out_weights.at[s], l_sems.at[CHUNKS, 0])])
    for copies in local:
        for copy in copies:
            copy.start()

    own_rows = pl.multiple_of(t * 64, 64)
    for i in range(4):
        rows = tokens[i * 16 : (i + 1) * 16, :].astype(F32)
        scale = lax.rsqrt(jnp.mean(rows * rows, axis=-1, keepdims=True) + 1e-06)
        normed[pl.ds(own_rows + i * 16, 16), :] = (rows * scale * gain[...]).astype(BF16)

    pl.semaphore_wait(barrier, len(partners))

    def token_rows(dx, dy, half=None):
        first = on_tp(dx, dy) * 64
        if half is None:
            return normed.at[pl.ds(pl.multiple_of(first, 64), 64)]
        return normed.at[pl.ds(pl.multiple_of(first + 32 * half, 32), 32)]

    def t_round(dx):
        rows = token_rows(dx, 0)
        send(rows, rows, t_sems.at[dx, 3, 0], tp_device(0, 1))
        send(rows, rows, t_sems.at[dx, 1, 0], tp_device(0, 3))

    def t_start():
        send(token_rows(0, 0), token_rows(0, 0), t_sems.at[1, 0, 0], tp_device(1, 0))
        t_round(0)

    def t_cross():
        arrived(token_rows(1, 0), t_sems.at[1, 0, 0])
        t_round(1)

    def t_pass(dx, dy):
        arrived(token_rows(dx, dy), t_sems.at[dx, dy, 0])
        half = 0 if dy == 3 else 1
        rows = token_rows(dx, dy, half)
        send(rows, rows, t_sems.at[dx, 2, half], tp_device(0, 4 - dy))

    def t_last(dx):
        for half in range(2):
            arrived(token_rows(dx, 2, half), t_sems.at[dx, 2, half])

    def shard(k, dz, dx, dc=0, half=None):
        origin = on_seq(dz, dx, dc)
        if k < CHUNKS:
            ref, depth = weights.at[k], 256
            first = origin * 256
        else:
            ref, depth = out_weights.at[origin], 512
            first = 0
        if half is None:
            return ref.at[pl.ds(pl.multiple_of(first, 256), depth)]
        return ref.at[pl.ds(pl.multiple_of(first + half * (depth // 2), 128), depth // 2)]

    def w_send(k, dz, dx, device, slot_dz, slot_dx, index=0, half=None):
        ref = shard(k, dz, dx, 0, half)
        send(ref, ref, w_sems.at[k, slot_dz, slot_dx, index], device)

    def w_arrived(k, dz, dx):
        if dz == 2 and (dx == 0 or k not in Z_FIRST):
            for half in range(2):
                arrived(shard(k, dz, dx, 0, half), w_sems.at[k, dz, dx, half])
        else:
            arrived(shard(k, dz, dx), w_sems.at[k, dz, dx, 0])

    def w_sibling(k, dz, dx):
        w_send(k, dz, dx, sibling, dz, dx, 2)

    def w_along_x(k, dz):
        w_send(k, dz, 0, seq_device(0, 1, 0), dz, 1)

    def w_round(k, dx):
        w_send(k, 0, dx, seq_device(1, 0, 0), 3, dx)
        w_send(k, 0, dx, seq_device(3, 0, 0), 1, dx)

    def w_pass(k, dz, dx):
        half = 0 if dz == 3 else 1
        w_send(k, dz, dx, seq_device(4 - dz, 0, 0), 2, dx, half, half)

    def w_own_x(k):
        if k not in loaded:
            loaded.append(k)
            for copy in local[k]:
                copy.wait()
        w_along_x(k, 0)

    def w_own_z(k):
        if k not in loaded:
            loaded.append(k)
            for copy in local[k]:
                copy.wait()
        w_round(k, 0)

    def w_x(k):
        w_arrived(k, 0, 1)
        w_round(k, 1)
        w_sibling(k, 0, 1)

    def w_z(k, dz):
        w_arrived(k, dz, 0)
        w_pass(k, dz, 0)
        if k in Z_FIRST:
            w_along_x(k, dz)
        w_sibling(k, dz, 0)

    def w_turn(k, dz):
        w_arrived(k, dz, 1)
        w_pass(k, dz, 1)
        w_sibling(k, dz, 1)

    def w_far(k, dx):
        w_arrived(k, 2, dx)
        if k in Z_FIRST:
            w_along_x(k, 2)
        w_sibling(k, 2, dx)

    def w_end(k, dz):
        w_arrived(k, dz, 1)
        w_sibling(k, dz, 1)

    def w_from_sibling(k, dz, dx):
        arrived(shard(k, dz, dx, 1), w_sems.at[k, dz, dx, 2])

    def w_ready(k):
        for dz in range(4):
            for dx in range(2):
                w_from_sibling(k, dz, dx)

    def half_of(side):
        return (xh + side) % 2

    def project(k, side):
        in_proj(normed, weights, wide, halo, k, half_of(side))

    def halo_send(k):
        send(halo.at[k, 0], halo.at[k, 1], h_sems.at[k], after)

    def feature(k):
        arrived(halo.at[k, 1], h_sems.at[k])
        featurize(short_ref, halo, wide, query, gate, k, s == 0)

    def conv(k, side):
        long_conv(gate, query, long_ref, skip_ref, mixed, k, half_of(side))

    groups = [(0, 0), (0, 1), (3, 0), (1, 0), (3, 1), (1, 1), (2, 0), (2, 1)]
    round_y = (2, 1, 3)

    def columns_of(g):
        return pl.ds(pl.multiple_of(on_seq(*groups[g], 0) // 2 * 512, 512), 512)

    def y_rows(dy):
        return pl.ds(pl.multiple_of((y + dy) % 4 * 64, 64), 64)

    def project_out(g, side):
        first = on_seq(*groups[g], 0) // 2 * 2
        half = half_of(side)

        def body(i, carry):
            origin = first + i
            rows = mixed[pl.ds(pl.multiple_of(half * 256, 256), 256), :]
            out = jnp.dot(rows, out_weights[origin], preferred_element_type=F32)
            part[half, :, pl.ds(pl.multiple_of(origin * 256, 256), 256)] = out.astype(BF16)
            return carry

        lax.fori_loop(0, 2, body, 0)

    def round_send(g, side, stage, slot):
        for dy in round_y:
            send(
                part.at[half_of(side), y_rows(dy), columns_of(g)],
                over_y.at[g, dy - 1, slot],
                r_sems.at[g, stage, dy - 1],
                tp_device(0, dy),
            )

    def round_arrived(g, stage, slot):
        for dy in round_y:
            arrived(over_y.at[g, dy - 1, slot], r_sems.at[g, stage, dy - 1])

    def emit(g, side):
        if side == 1:
            w_from_sibling(CHUNKS, *groups[g])
        project_out(g, side)
        if g not in RS_X_FIRST:
            round_send(g, side, 0 if side == 1 else 2, side)
        elif side == 1:
            send(part.at[half_of(1), :, columns_of(g)], over_x.at[g], r_sems.at[g, 0, 0], tp_device(1, 0))

    def stage_two(g):
        cols = columns_of(g)
        if g in RS_X_FIRST:
            arrived(over_x.at[g], r_sems.at[g, 0, 0])

            def body(i, carry):
                rows = pl.ds(pl.multiple_of(i * 64, 64), 64)
                both = part[xh, rows, cols].astype(F32) + over_x[g, rows, :].astype(F32)
                part[xh, rows, cols] = both.astype(BF16)
                return carry

            lax.fori_loop(0, 4, body, 0)
            round_send(g, 0, 1, 0)
        else:
            round_arrived(g, 0, 1)
            theirs = part[1 - xh, y_rows(0), cols].astype(F32)
            for dy in round_y:
                theirs = theirs + over_y[g, dy - 1, 1].astype(F32)
            part[1 - xh, y_rows(0), cols] = theirs.astype(BF16)
            send(part.at[1 - xh, y_rows(0), cols], over_x.at[g, pl.ds(0, 64)], r_sems.at[g, 1, 0], tp_device(1, 0))

    def finish(g):
        cols = columns_of(g)
        total = tokens[:, cols].astype(F32) + part[xh, y_rows(0), cols].astype(F32)
        round_arrived(g, 1 if g in RS_X_FIRST else 2, 0)
        for dy in round_y:
            total = total + over_y[g, dy - 1, 0].astype(F32)
        if g not in RS_X_FIRST:
            arrived(over_x.at[g, pl.ds(0, 64)], r_sems.at[g, 1, 0])
            total = total + over_x[g, 0:64, :].astype(F32)
        result[:, cols] = total.astype(BF16)

    t_start()
    w_own_z(0)
    w_sibling(0, 0, 0)
    w_own_z(1)
    w_sibling(1, 0, 0)
    w_own_z(2)
    w_sibling(2, 0, 0)
    w_own_z(3)
    w_sibling(3, 0, 0)
    w_own_x(0)
    w_z(0, 3)
    w_z(0, 1)
    w_own_x(1)
    w_z(1, 3)
    w_z(1, 1)
    w_own_x(2)
    t_pass(0, 3)
    t_pass(0, 1)
    t_cross()
    w_z(2, 3)
    w_z(2, 1)
    w_x(0)
    w_z(3, 3)
    w_z(3, 1)
    w_far(0, 0)
    t_last(0)
    w_x(1)
    w_far(1, 0)
    w_own_x(3)
    w_own_x(4)
    w_far(2, 0)
    w_end(2, 0)
    w_turn(0, 3)
    w_turn(0, 1)
    w_end(2, 3)
    w_far(3, 0)
    t_pass(1, 3)
    t_pass(1, 1)
    w_end(2, 1)
    w_turn(1, 3)
    w_turn(1, 1)
    w_far(0, 1)
    w_x(3)
    w_own_z(4)
    w_sibling(4, 0, 0)
    w_far(1, 1)
    w_ready(0)
    t_last(1)
    project(0, 0)
    project(0, 1)
    halo_send(0)
    w_ready(1)
    project(1, 1)
    w_turn(3, 3)
    w_turn(3, 1)
    project(1, 0)
    halo_send(1)
    feature(0)
    w_x(4)
    conv(0, 1)
    feature(1)
    conv(1, 1)
    w_end(2, 2)
    conv(0, 0)
    w_z(4, 3)
    w_z(4, 1)
    conv(1, 0)
    w_far(3, 1)
    w_ready(2)
    project(2, 0)
    project(2, 1)
    halo_send(2)
    w_ready(3)
    project(3, 0)
    project(3, 1)
    halo_send(3)
    feature(2)
    conv(2, 1)
    feature(3)
    conv(3, 1)
    emit(0, 1)
    emit(1, 1)
    w_turn(4, 3)
    w_turn(4, 1)
    emit(2, 1)
    emit(3, 1)
    conv(2, 0)
    conv(3, 0)
    w_far(4, 0)
    w_far(4, 1)
    emit(0, 0)
    emit(1, 0)
    stage_two(0)
    stage_two(1)
    emit(2, 0)
    emit(3, 0)
    emit(4, 1)
    emit(5, 1)
    emit(4, 0)
    emit(5, 0)
    emit(6, 1)
    emit(7, 1)
    emit(6, 0)
    emit(7, 0)
    stage_two(2)
    stage_two(3)
    finish(0)
    stage_two(4)
    stage_two(5)
    finish(1)
    stage_two(6)
    stage_two(7)
    finish(2)
    finish(3)
    finish(4)
    finish(5)
    finish(6)
    finish(7)
    for copy in started:
        copy.wait_send()


def on_device(tokens, norm_gain, in_weight, short_filter, long_filter, skip_gain, out_weight):
    channels = in_weight.shape[2]
    block = 512
    width = norm_gain.shape[0]
    vmem = pl.BlockSpec(memory_space=pltpu.VMEM)
    hbm = pl.BlockSpec(memory_space=pl.ANY)
    return pl.pallas_call(
        kernel,
        out_shape=jax.ShapeDtypeStruct(tokens.shape, BF16),
        in_specs=[vmem, vmem, hbm, vmem, vmem, vmem, hbm],
        out_specs=vmem,
        scratch_shapes=[
            pltpu.VMEM((block, width), BF16),
            pltpu.VMEM((CHUNKS, width, 3 * LANES), BF16),
            pltpu.VMEM((16, channels, 256), BF16),
            pltpu.VMEM((CHUNKS, 2, HALO, 3 * LANES), BF16),
            pltpu.VMEM((2, 3, HALO + block, LANES), F32),
            pltpu.VMEM((CHUNKS, block, LANES), F32),
            pltpu.VMEM((CHUNKS, block + 128, LANES), F32),
            pltpu.VMEM((block, channels), BF16),
            pltpu.VMEM((2, block // 2, width), BF16),
            pltpu.VMEM((8, block // 2, 512), BF16),
            pltpu.VMEM((8, 3, 2, 64, 512), BF16),
            pltpu.SemaphoreType.DMA((180,)),
            pltpu.SemaphoreType.DMA((CHUNKS + 1, 4, 2, 3)),
            pltpu.SemaphoreType.DMA((2, 4, 2)),
            pltpu.SemaphoreType.DMA((CHUNKS,)),
            pltpu.SemaphoreType.DMA((8, 3, 3)),
            pltpu.SemaphoreType.DMA((CHUNKS + 1, 3)),
        ],
        compiler_params=pltpu.CompilerParams(
            collective_id=0, has_side_effects=True, vmem_limit_bytes=58 * 2**20
        ),
        cost_estimate=pl.CostEstimate(flops=9_000_000_000, bytes_accessed=4_000_000, transcendentals=64),
    )(
        tokens,
        norm_gain.reshape(1, width),
        in_weight.transpose(1, 0, 2),
        short_filter.transpose(1, 0, 2),
        long_filter,
        skip_gain.reshape(1, channels),
        out_weight,
    )


def solution(mesh):
    placed = (
        P(("seq", "tp"), None),
        P(),
        P("seq", None, "tp"),
        P(None, None, "tp"),
        P(None, "tp"),
        P("tp"),
        P("tp", "seq"),
    )
    return jax.shard_map(
        on_device, mesh=mesh, in_specs=placed, out_specs=P(("seq", "tp"), None), check_vma=False
    )
```

```python
import functools

import jax
import jax.numpy as jnp
from jax import lax
from jax.experimental import pallas as pl
from jax.experimental.pallas import tpu as pltpu
from jax.sharding import PartitionSpec as P

MESH = pl.DeviceIdType.MESH
BF16 = jnp.bfloat16
F32 = jnp.float32

CHUNKS = 4
LANES = 128
HALO = 144
Z_FIRST = (2,)
RS_X_FIRST = (1, 3, 5, 7)


def in_proj(normed, weights, wide, halo, k, half):
    rows = normed.shape[0] // 2
    slot = k % 2
    at = pl.multiple_of(half * rows, rows)
    out = jnp.dot(normed[pl.ds(at, rows), :], weights[k], preferred_element_type=F32).astype(BF16)
    for p in range(3):
        wide[slot, p, pl.ds(pl.multiple_of(HALO + at, 8), rows), :] = out[:, p * LANES : (p + 1) * LANES].astype(F32)

    @pl.when(half == 1)
    def _():
        halo[k, 0] = out[rows - HALO :]


def featurize(short_ref, halo, wide, query, gate, k, first_block):
    block = query.shape[1]
    slot = k % 2
    keep = jnp.where(first_block, 0.0, 1.0).astype(F32)
    for p in range(3):
        wide[slot, p, 0:HALO, :] = halo[k, 1, :, p * LANES : (p + 1) * LANES].astype(F32) * keep
    taps = [[short_ref[p, j : j + 1, k * LANES : (k + 1) * LANES] for j in range(7)] for p in range(3)]

    def filt(p, first, rows):
        out = taps[p][0] * wide[slot, p, pl.ds(first, rows), :]
        for j in range(1, 7):
            out = out + taps[p][j] * wide[slot, p, pl.ds(first - j, rows), :]
        return out

    def gates(i, carry):
        at = pl.multiple_of(i * 64, 64)
        value = filt(1, 16 + at, 64) * filt(2, 16 + at, 64)
        gate[k, pl.ds(at, 64), :] = value.astype(BF16).astype(F32)
        return carry

    lax.fori_loop(0, (block + 128) // 64, gates, 0)

    def queries(i, carry):
        at = pl.multiple_of(i * 64, 64)
        query[k, pl.ds(at, 64), :] = filt(0, HALO + at, 64)
        return carry

    lax.fori_loop(0, block // 64, queries, 0)


def long_conv(gate, query, long_ref, skip_ref, mixed, k, half):
    columns = slice(k * LANES, (k + 1) * LANES)
    rows = query.shape[1] // 2
    tile = 128

    def body(i, carry):
        at = pl.multiple_of(half * rows + i * tile, tile)

        def eight_taps(group, total):
            first = pl.multiple_of(group * 8, 8)
            taps = long_ref[pl.ds(first, 8), columns]
            for b in range(8):
                total = total + taps[b : b + 1] * gate[k, pl.ds(128 + at - first - b, tile), :]
            return total

        total = skip_ref[:, columns] * gate[k, pl.ds(128 + at, tile), :]
        total = lax.fori_loop(0, long_ref.shape[0] // 8, eight_taps, total)
        mixed[pl.ds(at, tile), columns] = (query[k, pl.ds(at, tile), :] * total).astype(BF16)
        return carry

    lax.fori_loop(0, rows // tile, body, 0)


def kernel(
    tokens,
    gain,
    in_w,
    short_ref,
    long_ref,
    skip_ref,
    out_w,
    result,
    normed,
    weights,
    out_weights,
    halo,
    wide,
    query,
    gate,
    mixed,
    part,
    over_x,
    over_y,
    send_sems,
    w_sems,
    t_sems,
    h_sems,
    r_sems,
    l_sems,
):
    s, t = lax.axis_index("seq"), lax.axis_index("tp")
    z, xl, core = s // 4, (s // 2) % 2, s % 2
    xh, y = t // 4, t % 4

    def on_seq(dz, dx, dc):
        return ((z + dz) % 4) * 4 + ((xl + dx) % 2) * 2 + (core + dc) % 2

    def on_tp(dx, dy):
        return ((xh + dx) % 2) * 4 + (y + dy) % 4

    def seq_device(dz, dx, dc):
        return (on_seq(dz, dx, dc), t)

    def tp_device(dx, dy):
        return (s, on_tp(dx, dy))

    after = (lax.rem(s + 1, 16), t)
    before = (lax.rem(s + 15, 16), t)
    sibling = seq_device(0, 0, 1)

    partners = [sibling, seq_device(0, 1, 0), seq_device(1, 0, 0), seq_device(3, 0, 0), after, before]
    partners += [tp_device(dx, dy) for dx in range(2) for dy in range(4) if dx or dy]
    barrier = pltpu.get_barrier_semaphore()
    for partner in partners:
        pl.semaphore_signal(barrier, inc=1, device_id=partner, device_id_type=MESH)

    started, loaded = [], []

    def send(src, dst, recv_sem, device):
        copy = pltpu.make_async_remote_copy(
            src_ref=src,
            dst_ref=dst,
            send_sem=send_sems.at[len(started)],
            recv_sem=recv_sem,
            device_id=device,
            device_id_type=MESH,
        )
        copy.start()
        started.append(copy)

    def arrived(dst, recv_sem):
        pltpu.make_async_remote_copy(
            src_ref=dst,
            dst_ref=dst,
            send_sem=send_sems.at[0],
            recv_sem=recv_sem,
            device_id=sibling,
            device_id_type=MESH,
        ).wait_recv()

    local = []
    for k in range(CHUNKS):
        rows = weights.at[k, pl.ds(pl.multiple_of(s * 256, 256), 256)]
        local.append(
            [
                pltpu.make_async_copy(
                    in_w.at[p, :, pl.ds(k * LANES, LANES)], rows.at[:, pl.ds(p * LANES, LANES)], l_sems.at[k, p]
                )
                for p in range(3)
            ]
        )
    local.append([pltpu.make_async_copy(out_w, out_weights.at[s], l_sems.at[CHUNKS, 0])])
    for copies in local:
        for copy in copies:
            copy.start()

    own_rows = pl.multiple_of(t * 64, 64)
    for i in range(4):
        rows = tokens[i * 16 : (i + 1) * 16, :].astype(F32)
        scale = lax.rsqrt(jnp.mean(rows * rows, axis=-1, keepdims=True) + 1e-06)
        normed[pl.ds(own_rows + i * 16, 16), :] = (rows * scale * gain[...]).astype(BF16)

    pl.semaphore_wait(barrier, len(partners))

    def token_rows(dx, dy, half=None):
        first = on_tp(dx, dy) * 64
        if half is None:
            return normed.at[pl.ds(pl.multiple_of(first, 64), 64)]
        return normed.at[pl.ds(pl.multiple_of(first + 32 * half, 32), 32)]

    def t_round(dx):
        rows = token_rows(dx, 0)
        send(rows, rows, t_sems.at[dx, 3, 0], tp_device(0, 1))
        send(rows, rows, t_sems.at[dx, 1, 0], tp_device(0, 3))

    def t_start():
        send(token_rows(0, 0), token_rows(0, 0), t_sems.at[1, 0, 0], tp_device(1, 0))
        t_round(0)

    def t_cross():
        arrived(token_rows(1, 0), t_sems.at[1, 0, 0])
        t_round(1)

    def t_pass(dx, dy):
        arrived(token_rows(dx, dy), t_sems.at[dx, dy, 0])
        half = 0 if dy == 3 else 1
        rows = token_rows(dx, dy, half)
        send(rows, rows, t_sems.at[dx, 2, half], tp_device(0, 4 - dy))

    def t_last(dx):
        for half in range(2):
            arrived(token_rows(dx, 2, half), t_sems.at[dx, 2, half])

    def shard(k, dz, dx, dc=0, half=None):
        origin = on_seq(dz, dx, dc)
        if k < CHUNKS:
            ref, depth = weights.at[k], 256
            first = origin * 256
        else:
            ref, depth = out_weights.at[origin], 512
            first = 0
        if half is None:
            return ref.at[pl.ds(pl.multiple_of(first, 256), depth)]
        return ref.at[pl.ds(pl.multiple_of(first + half * (depth // 2), 128), depth // 2)]

    def w_send(k, dz, dx, device, slot_dz, slot_dx, index=0, half=None):
        ref = shard(k, dz, dx, 0, half)
        send(ref, ref, w_sems.at[k, slot_dz, slot_dx, index], device)

    def w_arrived(k, dz, dx):
        if dz == 2 and (dx == 0 or k not in Z_FIRST):
            for half in range(2):
                arrived(shard(k, dz, dx, 0, half), w_sems.at[k, dz, dx, half])
        else:
            arrived(shard(k, dz, dx), w_sems.at[k, dz, dx, 0])

    def w_sibling(k, dz, dx):
        w_send(k, dz, dx, sibling, dz, dx, 2)

    def w_along_x(k, dz):
        w_send(k, dz, 0, seq_device(0, 1, 0), dz, 1)

    def w_round(k, dx):
        w_send(k, 0, dx, seq_device(1, 0, 0), 3, dx)
        w_send(k, 0, dx, seq_device(3, 0, 0), 1, dx)

    def w_pass(k, dz, dx):
        half = 0 if dz == 3 else 1
        w_send(k, dz, dx, seq_device(4 - dz, 0, 0), 2, dx, half, half)

    def w_own_x(k):
        if k not in loaded:
            loaded.append(k)
            for copy in local[k]:
                copy.wait()
        w_along_x(k, 0)

    def w_own_z(k):
        if k not in loaded:
            loaded.append(k)
            for copy in local[k]:
                copy.wait()
        w_round(k, 0)

    def w_x(k):
        w_arrived(k, 0, 1)
        w_round(k, 1)
        w_sibling(k, 0, 1)

    def w_z(k, dz):
        w_arrived(k, dz, 0)
        w_pass(k, dz, 0)
        if k in Z_FIRST:
            w_along_x(k, dz)
        w_sibling(k, dz, 0)

    def w_turn(k, dz):
        w_arrived(k, dz, 1)
        w_pass(k, dz, 1)
        w_sibling(k, dz, 1)

    def w_far(k, dx):
        w_arrived(k, 2, dx)
        if k in Z_FIRST:
            w_along_x(k, 2)
        w_sibling(k, 2, dx)

    def w_end(k, dz):
        w_arrived(k, dz, 1)
        w_sibling(k, dz, 1)

    def w_from_sibling(k, dz, dx):
        arrived(shard(k, dz, dx, 1), w_sems.at[k, dz, dx, 2])

    def w_ready(k):
        for dz in range(4):
            for dx in range(2):
                w_from_sibling(k, dz, dx)

    def half_of(side):
        return (xh + side) % 2

    def project(k, side):
        in_proj(normed, weights, wide, halo, k, half_of(side))

    def halo_send(k):
        send(halo.at[k, 0], halo.at[k, 1], h_sems.at[k], after)

    def feature(k):
        arrived(halo.at[k, 1], h_sems.at[k])
        featurize(short_ref, halo, wide, query, gate, k, s == 0)

    def conv(k, side):
        long_conv(gate, query, long_ref, skip_ref, mixed, k, half_of(side))

    groups = [(0, 0), (0, 1), (3, 0), (1, 0), (3, 1), (1, 1), (2, 0), (2, 1)]
    round_y = (2, 1, 3)

    def columns_of(g):
        return pl.ds(pl.multiple_of(on_seq(*groups[g], 0) // 2 * 512, 512), 512)

    def y_rows(dy):
        return pl.ds(pl.multiple_of((y + dy) % 4 * 64, 64), 64)

    def project_out(g, side):
        first = on_seq(*groups[g], 0) // 2 * 2
        half = half_of(side)

        def body(i, carry):
            origin = first + i
            rows = mixed[pl.ds(pl.multiple_of(half * 256, 256), 256), :]
            out = jnp.dot(rows, out_weights[origin], preferred_element_type=F32)
            part[half, :, pl.ds(pl.multiple_of(origin * 256, 256), 256)] = out.astype(BF16)
            return carry

        lax.fori_loop(0, 2, body, 0)

    def round_send(g, side, stage, slot):
        for dy in round_y:
            send(
                part.at[half_of(side), y_rows(dy), columns_of(g)],
                over_y.at[g, dy - 1, slot],
                r_sems.at[g, stage, dy - 1],
                tp_device(0, dy),
            )

    def round_arrived(g, stage, slot):
        for dy in round_y:
            arrived(over_y.at[g, dy - 1, slot], r_sems.at[g, stage, dy - 1])

    def emit(g, side):
        if side == 1:
            w_from_sibling(CHUNKS, *groups[g])
        project_out(g, side)
        if g not in RS_X_FIRST:
            round_send(g, side, 0 if side == 1 else 2, side)
        elif side == 1:
            send(part.at[half_of(1), :, columns_of(g)], over_x.at[g], r_sems.at[g, 0, 0], tp_device(1, 0))

    def stage_two(g):
        cols = columns_of(g)
        if g in RS_X_FIRST:
            arrived(over_x.at[g], r_sems.at[g, 0, 0])

            def body(i, carry):
                rows = pl.ds(pl.multiple_of(i * 64, 64), 64)
                both = part[xh, rows, cols].astype(F32) + over_x[g, rows, :].astype(F32)
                part[xh, rows, cols] = both.astype(BF16)
                return carry

            lax.fori_loop(0, 4, body, 0)
            round_send(g, 0, 1, 0)
        else:
            round_arrived(g, 0, 1)
            theirs = part[1 - xh, y_rows(0), cols].astype(F32)
            for dy in round_y:
                theirs = theirs + over_y[g, dy - 1, 1].astype(F32)
            part[1 - xh, y_rows(0), cols] = theirs.astype(BF16)
            send(part.at[1 - xh, y_rows(0), cols], over_x.at[g, pl.ds(0, 64)], r_sems.at[g, 1, 0], tp_device(1, 0))

    def finish(g):
        cols = columns_of(g)
        total = tokens[:, cols].astype(F32) + part[xh, y_rows(0), cols].astype(F32)
        round_arrived(g, 1 if g in RS_X_FIRST else 2, 0)
        for dy in round_y:
            total = total + over_y[g, dy - 1, 0].astype(F32)
        if g not in RS_X_FIRST:
            arrived(over_x.at[g, pl.ds(0, 64)], r_sems.at[g, 1, 0])
            total = total + over_x[g, 0:64, :].astype(F32)
        result[:, cols] = total.astype(BF16)

    t_start()
    w_own_z(0)
    w_sibling(0, 0, 0)
    w_own_z(1)
    w_sibling(1, 0, 0)
    w_own_z(2)
    w_sibling(2, 0, 0)
    w_own_z(3)
    w_sibling(3, 0, 0)
    w_own_x(0)
    w_z(0, 3)
    w_z(0, 1)
    w_own_x(1)
    w_z(1, 3)
    w_z(1, 1)
    w_own_x(2)
    t_pass(0, 3)
    t_pass(0, 1)
    t_cross()
    w_z(2, 3)
    w_z(2, 1)
    w_x(0)
    w_z(3, 3)
    w_z(3, 1)
    w_far(0, 0)
    t_last(0)
    w_x(1)
    w_far(1, 0)
    w_own_x(3)
    w_own_x(4)
    w_far(2, 0)
    w_end(2, 0)
    w_turn(0, 3)
    w_turn(0, 1)
    w_end(2, 3)
    w_far(3, 0)
    t_pass(1, 3)
    t_pass(1, 1)
    w_end(2, 1)
    w_turn(1, 3)
    w_turn(1, 1)
    w_far(0, 1)
    w_x(3)
    w_own_z(4)
    w_sibling(4, 0, 0)
    w_far(1, 1)
    w_ready(0)
    t_last(1)
    project(0, 0)
    project(0, 1)
    halo_send(0)
    w_ready(1)
    project(1, 1)
    w_turn(3, 3)
    w_turn(3, 1)
    project(1, 0)
    halo_send(1)
    feature(0)
    w_x(4)
    conv(0, 1)
    feature(1)
    conv(1, 1)
    w_end(2, 2)
    conv(0, 0)
    conv(1, 0)
    w_far(3, 1)
    w_ready(2)
    project(2, 0)
    project(2, 1)
    halo_send(2)
    w_ready(3)
    project(3, 0)
    project(3, 1)
    halo_send(3)
    w_z(4, 3)
    w_z(4, 1)
    feature(2)
    conv(2, 1)
    feature(3)
    conv(3, 1)
    emit(0, 1)
    emit(1, 1)
    w_turn(4, 3)
    w_turn(4, 1)
    emit(2, 1)
    emit(3, 1)
    conv(2, 0)
    conv(3, 0)
    w_far(4, 0)
    w_far(4, 1)
    emit(0, 0)
    emit(1, 0)
    stage_two(0)
    stage_two(1)
    emit(2, 0)
    emit(3, 0)
    emit(4, 1)
    emit(5, 1)
    emit(4, 0)
    emit(5, 0)
    emit(6, 1)
    emit(7, 1)
    emit(6, 0)
    emit(7, 0)
    stage_two(2)
    stage_two(3)
    finish(0)
    stage_two(4)
    stage_two(5)
    finish(1)
    stage_two(6)
    stage_two(7)
    finish(2)
    finish(3)
    finish(4)
    finish(5)
    finish(6)
    finish(7)
    for copy in started:
        copy.wait_send()


def on_device(tokens, norm_gain, in_weight, short_filter, long_filter, skip_gain, out_weight):
    channels = in_weight.shape[2]
    block = 512
    width = norm_gain.shape[0]
    vmem = pl.BlockSpec(memory_space=pltpu.VMEM)
    hbm = pl.BlockSpec(memory_space=pl.ANY)
    return pl.pallas_call(
        kernel,
        out_shape=jax.ShapeDtypeStruct(tokens.shape, BF16),
        in_specs=[vmem, vmem, hbm, vmem, vmem, vmem, hbm],
        out_specs=vmem,
        scratch_shapes=[
            pltpu.VMEM((block, width), BF16),
            pltpu.VMEM((CHUNKS, width, 3 * LANES), BF16),
            pltpu.VMEM((16, channels, 256), BF16),
            pltpu.VMEM((CHUNKS, 2, HALO, 3 * LANES), BF16),
            pltpu.VMEM((2, 3, HALO + block, LANES), F32),
            pltpu.VMEM((CHUNKS, block, LANES), F32),
            pltpu.VMEM((CHUNKS, block + 128, LANES), F32),
            pltpu.VMEM((block, channels), BF16),
            pltpu.VMEM((2, block // 2, width), BF16),
            pltpu.VMEM((8, block // 2, 512), BF16),
            pltpu.VMEM((8, 3, 2, 64, 512), BF16),
            pltpu.SemaphoreType.DMA((180,)),
            pltpu.SemaphoreType.DMA((CHUNKS + 1, 4, 2, 3)),
            pltpu.SemaphoreType.DMA((2, 4, 2)),
            pltpu.SemaphoreType.DMA((CHUNKS,)),
            pltpu.SemaphoreType.DMA((8, 3, 3)),
            pltpu.SemaphoreType.DMA((CHUNKS + 1, 3)),
        ],
        compiler_params=pltpu.CompilerParams(
            collective_id=0, has_side_effects=True, vmem_limit_bytes=58 * 2**20
        ),
        cost_estimate=pl.CostEstimate(flops=9_000_000_000, bytes_accessed=4_000_000, transcendentals=64),
    )(
        tokens,
        norm_gain.reshape(1, width),
        in_weight.transpose(1, 0, 2),
        short_filter.transpose(1, 0, 2),
        long_filter,
        skip_gain.reshape(1, channels),
        out_weight,
    )


def solution(mesh):
    placed = (
        P(("seq", "tp"), None),
        P(),
        P("seq", None, "tp"),
        P(None, None, "tp"),
        P(None, "tp"),
        P("tp"),
        P("tp", "seq"),
    )
    return jax.shard_map(
        on_device, mesh=mesh, in_specs=placed, out_specs=P(("seq", "tp"), None), check_vma=False
    )
```
